256 devices in a mesh: arc: 32 (over x_lo, z, core), col: 8 (over y, x_hi).
Axes of the slice: x: 4 (x_hi: 2, x_lo: 2; x = x_hi * 2 + x_lo), y: 4, z: 8, core: 2. Of those that a mesh axis runs over, the one named last changes fastest.
Arguments:
- force: float32 [3, 2048, 15360], P(None, 'arc', 'col'), may hold values from -0.8 to 0.8
- propagate: float32 [6, 6, 2048], P(None, None, 'arc'), may hold values from -0.02 to 1
- sight: float32 [6, 2048], P(None, 'arc'), may hold values from -2.4 to 2.4
- weights: float32 [2048], P('arc'), may hold values from 0.2 to 2
- lengths: int32 [32], replicated, may hold values from 1 to 192, 2048 in all
- order: int32 [32], replicated, may hold values from 0 to 31, each once
Outputs:
- normal: float32 [15360, 15360], P('arc', 'col')
The draws below stay inside these ranges and needn't reach their ends.
Inputs may be any that keep to these rules, and one draw needn't show every extreme that they name: The lengths sum to 2048. `order`: each block number once.
All inputs are finite; a program needn't handle non-finite values.
Results may differ from the reference program's by a relative error of at most 0.00014.
Values sent between devices are 32-bit elements; how exact they have to be, the bound alone decides.
No kernel may reach another device: no remote copies, remote signals or barrier semaphores. Data moves between devices by JAX's collectives and lax.ppermute only.
A program may use at most 128 MiB of HBM per device.

```python
import math
import jax
import jax.numpy as jnp
import numpy as np
from jax import lax

K = 15360
EP_DEV = 64
WINDOW_EPOCHS = 2048
ARCS = 32
SPAN = 192
N_ARC = 32


def draw_propagate(key, part):
    key = jax.random.fold_in(key, 11)
    first, second, third_term, fourth_term, fifth = jax.random.split(key, 5)
    speed = jnp.exp(jax.random.uniform(first, (6,), jnp.float32, math.log(0.3), math.log(40.0)))
    device_factor = jnp.exp(jax.random.uniform(second, (WINDOW_EPOCHS // EP_DEV,), jnp.float32, math.log(0.7), math.log(1.5)))
    per_epoch = jnp.repeat(device_factor, EP_DEV, total_repeat_length=WINDOW_EPOCHS)
    rate = speed[:, None] * per_epoch[None, :] / EP_DEV
    cluster_positions = jax.random.randint(third_term, (4,), 0, WINDOW_EPOCHS)
    epoch_cluster = jnp.any(jnp.arange(WINDOW_EPOCHS)[None, :] == cluster_positions[:, None], axis=0)
    split_point = jnp.where(epoch_cluster, jax.random.uniform(fourth_term, (WINDOW_EPOCHS,), jnp.float32, 0.5, 0.8), 1.0)
    diagonal = jnp.exp(-rate) * split_point[None, :]
    matrix = jnp.eye(6, dtype=jnp.float32)[:, :, None] * diagonal[None, :, :]
    coupling = jax.random.uniform(fifth, (3, 3, WINDOW_EPOCHS), jnp.float32, -0.02, 0.02)
    matrix = matrix.at[0:3, 3:6, :].set(coupling)
    return matrix.astype(jnp.float32)


def shard_levels(rng, shape, cuts, least, largest):
    level, own = 1.0, jax.random.fold_in(rng, 6)
    for axis_at, parts in cuts:
        heights = jnp.exp(jax.random.uniform(jax.random.fold_in(own, axis_at), (parts,), jnp.float32, least / len(cuts), largest / len(cuts)))
        level = level * jnp.repeat(heights, shape[axis_at] // parts).reshape([-1 if axis == axis_at else 1 for axis in range(len(shape))])
    return level


def profile(amount, total, bound, lean):
    portions = [(1 << 20) // math.isqrt(standing ** lean) + 1 for standing in range(2, amount + 1)]
    surplus, holding = total - bound - (amount - 1), [1] * (amount - 1)
    while surplus > 0:
        candidates = [i for i in range(amount - 1) if holding[i] < bound]
        pool, budget = sum([portions[i] for i in candidates]), surplus
        for i in candidates:
            extra = min(bound - holding[i], max(1, budget * portions[i] // pool), surplus)
            holding[i] = holding[i] + extra
            surplus = surplus - extra
    return np.array([bound] + holding)


def ragged(stream_key, amount, total, bound, lean):
    if amount == 2:
        one = jax.random.randint(stream_key, (), max(1, total - bound), min(bound, total - 1) + 1)
        return jnp.stack([one, total - one])
    tallies = jnp.asarray(profile(amount, total, bound, lean), jnp.int32)
    pairs = (amount - 1) // 2
    source_of, receiver = tallies[1:1 + 2 * pairs:2], tallies[2:2 + 2 * pairs:2]
    room = jnp.minimum(source_of - 1, bound - receiver)
    shifted = jax.random.randint(jax.random.fold_in(stream_key, 1), (pairs,), 0, 1 << 20) % (room + 1)
    tallies = tallies.at[1:1 + 2 * pairs:2].set(source_of - shifted).at[2:2 + 2 * pairs:2].set(receiver + shifted)
    return tallies[jax.random.permutation(jax.random.fold_in(stream_key, 2), amount)]


def noise(own_key, dims, width, bound, cuts=(), kind=jnp.bfloat16):
    gain = shard_levels(own_key, dims, cuts, -0.22, 0.18) if cuts else 1.0
    array = jax.random.normal(own_key, dims, jnp.float32) * width * gain
    return jnp.minimum(jnp.maximum(array, -bound), bound).astype(kind)


def setup_inputs(seed: int = 0) -> dict:
    keys = jax.random.split(jax.random.key(seed), 7)
    return {
        "force": noise(keys[0], (3, WINDOW_EPOCHS, K), 0.1, 0.8, ((1, 32), (2, 8)), jnp.float32),
        "propagate": draw_propagate(jax.random.fold_in(keys[6], 71), 0),
        "sight": noise(keys[2], (6, WINDOW_EPOCHS), 0.4, 2.4, ((1, 32),), jnp.float32),
        "weights": jnp.clip(jnp.exp(math.log(2.0) - 2.3025851 * jax.random.uniform(keys[3], (WINDOW_EPOCHS,), jnp.float32) ** shard_levels(keys[3], (WINDOW_EPOCHS,), ((0, 32),), -0.2, 0.2)), 0.2, 2.0),
        "lengths": ragged(keys[4], ARCS, WINDOW_EPOCHS, SPAN, 2).astype(jnp.int32),
        "order": jax.random.permutation(keys[5], N_ARC).astype(jnp.int32),
    }


def reference(force, propagate, sight, weights, lengths, order):
    high = lax.Precision.HIGHEST
    epochs = force.shape[1]
    starts = jnp.cumsum(lengths) - lengths
    positions = jnp.arange(epochs, dtype=jnp.int32)
    fresh = jnp.any(positions[:, None] == starts[None, :].astype(jnp.int32), axis=1)
    keep = jnp.where(fresh, 1.0, 0.0)
    keep = (1.0 - keep).astype(jnp.float32)
    transfer = jnp.moveaxis(propagate, 2, 0) * keep[:, None, None]
    partials = jnp.moveaxis(force, 1, 0)
    looking = jnp.moveaxis(sight, 1, 0)

    def advance(state, inputs):
        matrix, kick, line = inputs
        state = jnp.dot(matrix, state, precision=high) + jnp.concatenate([0.5 * kick, kick], 0)
        return state, jnp.dot(line, state, precision=high)

    start_state = jnp.zeros((6, force.shape[2]), jnp.float32)
    _, design = lax.scan(advance, start_state, (transfer, partials, looking))
    weighted = design * (weights / epochs)[:, None]
    blocks = weighted.reshape(epochs, N_ARC, K // N_ARC)[:, order, :].reshape(epochs, K)
    return lax.dot_general(blocks, design, (((0,), (0,)), ((), ())), precision=high, preferred_element_type=jnp.float32)
```

```python
import functools

import jax
import jax.numpy as jnp
from jax import lax
from jax.experimental import pallas as pl
from jax.experimental.pallas import tpu as pltpu
from jax.sharding import PartitionSpec as P

HIGH = lax.Precision.HIGHEST
AXES = ("arc", "col")
XL, NZ, CO, NY, XH = 2, 8, 2, 4, 2
EPOCHS = 64
SLOTS = 8
WIDE = 1920
BLOCK = 480
EVERY = 2048
LAST = [(2, 0), (2, 1)]
EARLY = [(dy, dxh) for dy in (0, 1, 3) for dxh in range(XH)]
LATE = (NZ + 3, NZ + 4, NZ + 5, NZ + 6)
DEEP = 128 * len(LAST)
PICK = SLOTS * len(LATE) * len(EARLY)
MIB = 1 << 20
WHOLE = 60 * MIB
VMEM = pl.BlockSpec(memory_space=pltpu.VMEM)
SMEM = pl.BlockSpec(memory_space=pltpu.SMEM)
HBM = pl.BlockSpec(memory_space=pltpu.HBM)


def place(device):
    arc, col = divmod(device, NY * XH)
    xl, rest = divmod(arc, NZ * CO)
    z, core = divmod(rest, CO)
    y, xh = divmod(col, XH)
    return xl, z, core, y, xh


def number(xl, z, core, y, xh):
    return (((xl * NZ + z) * CO + core) * NY + y) * XH + xh


def send(value, dxl=0, dz=0, dcore=0, dy=0, dxh=0):
    pairs = []
    for device in range(XL * NZ * CO * NY * XH):
        xl, z, core, y, xh = place(device)
        there = number(xl ^ dxl, (z + dz) % NZ, core ^ dcore, (y + dy) % NY, xh ^ dxh)
        pairs.append((device, there))
    return lax.ppermute(value, AXES, pairs)


def coordinates():
    arc, col = lax.axis_index("arc"), lax.axis_index("col")
    xl, z, core = arc // (NZ * CO), (arc // CO) % NZ, arc % CO
    return xl, z, core, col // XH, col % XH


def scan_kernel(
    lengths_hbm, propagate_hbm, sight_hbm, weights_hbm, force_hbm,
    pack, coef, flat,
    lengths, propagate, sight, weights, keep, last, sems,
):
    loads = [
        pltpu.make_async_copy(force_hbm, flat, sems.at[0]),
        pltpu.make_async_copy(lengths_hbm, lengths, sems.at[1]),
        pltpu.make_async_copy(propagate_hbm, propagate, sems.at[2]),
        pltpu.make_async_copy(sight_hbm, sight, sems.at[3]),
        pltpu.make_async_copy(weights_hbm, weights, sems.at[4]),
    ]
    for load in loads:
        load.start()
    rank = lax.axis_index("arc")

    def clear(t, _):
        keep[t] = 1.0
        return 0

    lax.fori_loop(0, EPOCHS, clear, 0)
    loads[1].wait()

    def mark(arc, start):
        local = start - rank * EPOCHS

        @pl.when((local >= 0) & (local < EPOCHS))
        def _():
            keep[local] = 0.0

        return start + lengths[arc]

    lax.fori_loop(0, lengths.shape[0], mark, jnp.int32(0))
    lane = lax.broadcasted_iota(jnp.int32, (1, 256), 1)
    rows = tuple((lane == 192 + i).astype(jnp.float32) for i in range(6))
    loads[2].wait()
    loads[3].wait()
    loads[4].wait()

    def step(t, rows):
        live = keep[t]
        kicked = []
        for i in range(6):
            total = propagate[i, 0, t] * rows[0]
            for j in range(1, 6):
                total = total + propagate[i, j, t] * rows[j]
            kick = jnp.where(lane == (i % 3) * EPOCHS + t, 0.5 if i < 3 else 1.0, 0.0)
            kicked.append(live * total + kick)
        seen = sight[0, t] * kicked[0]
        for i in range(1, 6):
            seen = seen + sight[i, t] * kicked[i]
        coef[pl.ds(t, 1), :] = jnp.where(lane == 200, weights[t] / EVERY, seen)
        return tuple(kicked)

    rows = lax.fori_loop(0, EPOCHS, step, rows, unroll=4)
    last[...] = jnp.zeros_like(last)
    for i in range(6):
        last[i : i + 1, :] = rows[i]
    loads[0].wait()
    pack[:, :WIDE] = jnp.dot(
        last[:, : 3 * EPOCHS],
        flat[...].reshape(3 * EPOCHS, WIDE),
        precision=HIGH,
        preferred_element_type=jnp.float32,
    )
    pack[:, WIDE:] = last[:, 128:]


def scan(lengths, propagate, sight, weights, force):
    return pl.pallas_call(
        scan_kernel,
        out_shape=(
            jax.ShapeDtypeStruct((8, WIDE + 128), jnp.float32),
            jax.ShapeDtypeStruct((EPOCHS, 256), jnp.float32),
            jax.ShapeDtypeStruct(force.shape, jnp.float32),
        ),
        in_specs=[HBM] * 5,
        out_specs=(VMEM, VMEM, VMEM),
        scratch_shapes=[
            pltpu.SMEM(lengths.shape, jnp.int32),
            pltpu.SMEM(propagate.shape, jnp.float32),
            pltpu.SMEM(sight.shape, jnp.float32),
            pltpu.SMEM(weights.shape, jnp.float32),
            pltpu.SMEM((EPOCHS,), jnp.float32),
            pltpu.VMEM((8, 256), jnp.float32),
            pltpu.SemaphoreType.DMA((5,)),
        ],
        compiler_params=pltpu.CompilerParams(vmem_limit_bytes=WHOLE),
        name="scan",
    )(lengths, propagate, sight, weights, force)


def local_kernel(coef, flat, design):
    design[...] = jnp.dot(
        coef[:, : 3 * EPOCHS],
        flat[...].reshape(3 * EPOCHS, WIDE),
        precision=HIGH,
        preferred_element_type=jnp.float32,
    )


def local_design(coef, flat):
    return pl.pallas_call(
        local_kernel,
        out_shape=jax.ShapeDtypeStruct((EPOCHS, WIDE), jnp.float32),
        in_specs=[VMEM, VMEM],
        out_specs=VMEM,
        compiler_params=pltpu.CompilerParams(vmem_limit_bytes=16 * MIB),
        cost_estimate=pl.CostEstimate(flops=300_000_000, bytes_accessed=2_000_000, transcendentals=0),
        name="local",
    )(coef, flat)


def apply(matrix, state):
    total = matrix[:, 0:1] * state[0:1, :]
    for j in range(1, 6):
        total = total + matrix[:, j : j + 1] * state[j : j + 1, :]
    return total


def design_kernel(one, two, three, coef, local, design, keep, cross, weighted):
    state = three[:, :WIDE]
    for earlier in (two, one):
        state = apply(earlier[:, WIDE + 64 : WIDE + 70], state) + earlier[:, :WIDE]
    full = local[...] + apply(coef[:, 192:198], state)
    design[...] = full
    weighted[...] = full * coef[:, 200:201]
    _, _, _, y, xh = coordinates()
    for dy in range(NY):
        for dxh, out in enumerate((keep, cross)):
            slot = lax.rem(y + dy, NY) * XH + lax.rem(xh + dxh, XH)
            out[dy] = weighted[pl.ds(pl.multiple_of(slot * SLOTS, SLOTS), SLOTS), :]


def full_design(one, two, three, coef, local):
    pieces = jax.ShapeDtypeStruct((NY, SLOTS, WIDE), jnp.float32)
    return pl.pallas_call(
        design_kernel,
        out_shape=(jax.ShapeDtypeStruct((EPOCHS, WIDE), jnp.float32), pieces, pieces),
        in_specs=[VMEM] * 5,
        out_specs=(VMEM, VMEM, VMEM),
        scratch_shapes=[pltpu.VMEM((EPOCHS, WIDE), jnp.float32)],
        compiler_params=pltpu.CompilerParams(vmem_limit_bytes=16 * MIB),
        name="design",
    )(one, two, three, coef, local)


def pair_kernel(first, second, *outs):
    for i, out in enumerate(outs):
        out[0] = first[i]
        out[1] = second[i]


def pair(first, second):
    out = jax.ShapeDtypeStruct((2,) + first.shape[1:], jnp.float32)
    return pl.pallas_call(
        pair_kernel,
        out_shape=(out,) * first.shape[0],
        in_specs=[VMEM, VMEM],
        out_specs=(VMEM,) * first.shape[0],
        compiler_params=pltpu.CompilerParams(vmem_limit_bytes=16 * MIB),
        cost_estimate=pl.CostEstimate(flops=5_000_000_000, bytes_accessed=1_000_000, transcendentals=0),
        name="pair",
    )(first, second)


def choose_kernel(order, *refs):
    pieces, out, blocks = refs[:4], refs[4], refs[5]
    _, _, core, y, xh = coordinates()
    for dy in range(NY):
        for dxh in range(XH):
            col = lax.rem(y + dy, NY) * XH + lax.rem(xh + dxh, XH)
            for j in range(4):
                blocks[4 * col + j] = pieces[dy][dxh, :, BLOCK * j : BLOCK * (j + 1)]
    for chip in range(XL * NZ):
        for dcore in range(CO):
            out[chip, dcore] = blocks[order[chip * CO + lax.rem(core + dcore, CO)]]


def choose(order, pieces):
    return pl.pallas_call(
        choose_kernel,
        out_shape=jax.ShapeDtypeStruct((XL * NZ, CO, SLOTS, BLOCK), jnp.float32),
        in_specs=[SMEM] + [VMEM] * 4,
        out_specs=VMEM,
        scratch_shapes=[pltpu.VMEM((32, SLOTS, BLOCK), jnp.float32)],
        compiler_params=pltpu.CompilerParams(vmem_limit_bytes=16 * MIB),
        name="choose",
    )(order, *pieces)


def turn_kernel(pieces, out, gathered):
    xl, z, _, _, _ = coordinates()
    for dcore in range(CO):
        for dxl in range(XL):
            for dz in range(NZ):
                chip = lax.rem(xl + dxl, XL) * NZ + lax.rem(z + dz, NZ)
                start = SLOTS * (dxl * NZ + dz)
                gathered[start : start + SLOTS, :BLOCK] = pieces[chip, dcore]
        out[BLOCK * dcore : BLOCK * (dcore + 1), :] = jnp.transpose(gathered[...])[:BLOCK]


def turn(pieces):
    return pl.pallas_call(
        turn_kernel,
        out_shape=jax.ShapeDtypeStruct((CO * BLOCK, 128), jnp.float32),
        in_specs=[VMEM],
        out_specs=VMEM,
        scratch_shapes=[pltpu.VMEM((128, 512), jnp.float32)],
        compiler_params=pltpu.CompilerParams(vmem_limit_bytes=16 * MIB),
        name="turn",
    )(pieces)


def split(value):
    high = value.astype(jnp.bfloat16)
    return high, (value - high.astype(jnp.float32)).astype(jnp.bfloat16)


def stack_kernel(*refs):
    left, out = refs[:-1], refs[-1]
    depth = 128 * len(left)
    for j, shard in enumerate(left):
        high, low = split(shard[...])
        for part, value in enumerate((high, low, high)):
            out[:, depth * part + 128 * j : depth * part + 128 * (j + 1)] = value


def stack_early(left):
    return pl.pallas_call(
        stack_kernel,
        out_shape=jax.ShapeDtypeStruct((CO * BLOCK, 3 * 128 * len(left)), jnp.bfloat16),
        in_specs=[VMEM] * len(left),
        out_specs=VMEM,
        compiler_params=pltpu.CompilerParams(vmem_limit_bytes=12 * MIB),
        name="stack",
    )(*left)


def pick_kernel(*refs):
    left, out = refs[:-1], refs[-1]
    lanes = slice(SLOTS * LATE[0], SLOTS * (LATE[-1] + 1))
    value = jnp.concatenate([shard[:, lanes] for shard in left], axis=1)
    high = value.astype(jnp.bfloat16).astype(jnp.float32)
    out[...] = jnp.concatenate([high, value - high, high], axis=1).astype(jnp.bfloat16)


def pick_late(left):
    return pl.pallas_call(
        pick_kernel,
        out_shape=jax.ShapeDtypeStruct((CO * BLOCK, 3 * PICK), jnp.bfloat16),
        in_specs=[VMEM] * len(left),
        out_specs=VMEM,
        compiler_params=pltpu.CompilerParams(vmem_limit_bytes=12 * MIB),
        name="pick",
    )(*left)


def bring_kernel(*refs):
    half = len(refs) // 2
    for source, target in zip(refs[:half], refs[half:]):
        target[...] = source[...]


def bring(values):
    return pl.pallas_call(
        bring_kernel,
        out_shape=tuple(jax.ShapeDtypeStruct(value.shape, value.dtype) for value in values),
        in_specs=[VMEM] * len(values),
        out_specs=(VMEM,) * len(values),
        compiler_params=pltpu.CompilerParams(vmem_limit_bytes=12 * MIB),
        name="bring",
    )(*values)


def slot_rows(dy, dxh):
    _, _, _, y, xh = coordinates()
    slot = lax.rem(y + dy, NY) * XH + lax.rem(xh + dxh, XH)
    return pl.ds(pl.multiple_of(slot * SLOTS, SLOTS), SLOTS)


def early_kernel(lo, hi, left, *refs):
    right, outs, stacked = refs[:12], refs[12:14], refs[14]
    depth = 128 * len(EARLY)
    none = jnp.zeros((SLOTS * len(LATE), hi - lo), jnp.float32)
    for j, place in enumerate(EARLY):
        rows = slot_rows(*place)
        chunk = [block[rows, lo:hi] for block in right]
        high, low = split(jnp.concatenate(chunk[: LATE[0]] + [none] + chunk[LATE[0] :], axis=0))
        for part, value in enumerate((high, high, low)):
            stacked[depth * part + 128 * j : depth * part + 128 * (j + 1), :] = value
    for i, out in enumerate(outs):
        out[...] = jnp.dot(
            left[BLOCK * i : BLOCK * (i + 1), :], stacked[...], preferred_element_type=jnp.float32
        )


def early_product(left, right, lo, hi):
    out = jax.ShapeDtypeStruct((BLOCK, hi - lo), jnp.float32)
    depth = 128 * len(EARLY)
    return pl.pallas_call(
        functools.partial(early_kernel, lo, hi),
        out_shape=(out, out),
        in_specs=[VMEM] * 13,
        out_specs=(VMEM, VMEM),
        scratch_shapes=[pltpu.VMEM((3 * depth, hi - lo), jnp.bfloat16)],
        compiler_params=pltpu.CompilerParams(vmem_limit_bytes=14 * MIB),
        cost_estimate=pl.CostEstimate(
            flops=12 * BLOCK * depth * (hi - lo), bytes_accessed=14_000_000, transcendentals=0
        ),
        name="early",
    )(left, *right)


def late_kernel(lo, hi, first, second, picked, *refs):
    right, sums, outs, across, stacked = refs[:16], refs[16:18], refs[18:20], refs[20], refs[21]
    for j, (place, shard) in enumerate(zip(LAST, (first, second))):
        high, low = split(shard[...])
        for part, value in enumerate((high, low, high)):
            across[:, DEEP * part + 128 * j : DEEP * part + 128 * (j + 1)] = value
        rows = slot_rows(*place)
        high, low = split(jnp.concatenate([block[rows, lo:hi] for block in right], axis=0))
        for part, value in enumerate((high, high, low)):
            stacked[DEEP * part + 128 * j : DEEP * part + 128 * (j + 1), :] = value
    across[:, 3 * DEEP :] = picked[...]
    pieces = [right[i][slot_rows(*place), lo:hi] for place in EARLY for i in LATE]
    high, low = split(jnp.concatenate(pieces, axis=0))
    for part, value in enumerate((high, high, low)):
        stacked[3 * DEEP + PICK * part : 3 * DEEP + PICK * (part + 1), :] = value
    for i, out in enumerate(outs):
        out[...] = sums[i][...] + jnp.dot(
            across[BLOCK * i : BLOCK * (i + 1), :], stacked[...], preferred_element_type=jnp.float32
        )


def late_product(left, picked, right, lo, hi, sums):
    out = jax.ShapeDtypeStruct((BLOCK, hi - lo), jnp.float32)
    depth = 3 * (DEEP + PICK)
    return pl.pallas_call(
        functools.partial(late_kernel, lo, hi),
        out_shape=(out, out),
        in_specs=[VMEM] * 21,
        out_specs=(VMEM, VMEM),
        scratch_shapes=[
            pltpu.VMEM((CO * BLOCK, depth), jnp.bfloat16),
            pltpu.VMEM((depth, hi - lo), jnp.bfloat16),
        ],
        compiler_params=pltpu.CompilerParams(vmem_limit_bytes=14 * MIB),
        cost_estimate=pl.CostEstimate(
            flops=4 * BLOCK * depth * (hi - lo), bytes_accessed=14_000_000, transcendentals=0
        ),
        name="late",
    )(*left, picked, *right, *sums)


def finish_kernel(lo, hi, mine, passed, *refs):
    out, total, sem = refs[-3:]
    total[...] = mine[...] + passed[...]
    copy = pltpu.make_async_copy(total, out.at[:, lo:hi], sem)
    copy.start()
    copy.wait()


def finish(mine, passed, lo, hi, whole=None):
    given = () if whole is None else (whole,)
    return pl.pallas_call(
        functools.partial(finish_kernel, lo, hi),
        out_shape=jax.ShapeDtypeStruct((BLOCK, WIDE), jnp.float32),
        in_specs=[VMEM, VMEM] + [HBM] * len(given),
        out_specs=HBM,
        scratch_shapes=[pltpu.VMEM((BLOCK, hi - lo), jnp.float32), pltpu.SemaphoreType.DMA],
        input_output_aliases={2: 0} if given else {},
        compiler_params=pltpu.CompilerParams(vmem_limit_bytes=16 * MIB),
        name="finish",
    )(mine, passed, *given)


def shift_arc(value, step):
    arcs, cols = XL * NZ * CO, NY * XH
    pairs = [
        (arc * cols + col, (arc + step) * cols + col)
        for arc in range(arcs - step)
        for col in range(cols)
    ]
    return lax.ppermute(value, AXES, pairs)


def body(force, propagate, sight, weights, lengths, order):
    tie = lax.optimization_barrier
    pack, coef, flat = scan(lengths, propagate, sight, weights, force)
    before = [shift_arc(pack, step) for step in (1, 2, 3)]
    design, keep, cross = full_design(*before, coef, local_design(coef, flat))
    own, far = {0: design}, {}
    got, beside = tie((send(cross, dxh=1), own[0]))
    own[-1], own[1] = send(own[0], dz=1), send(own[0], dz=-1)
    to = pair(keep, got)
    rows = [to[0], send(to[3], dy=-1), send(to[2], dy=2), send(to[1], dy=1)]
    rows, own = tie((rows, own))
    own[-2], own[2] = send(own[-1], dz=1), send(own[1], dz=-1)
    third = send(own[-2], dz=1), send(own[2], dz=-1)
    far[0], beside = tie((send(beside, dxl=1), own[1]))
    second = send(beside, dxl=1)
    chosen = choose(order, rows)
    same_core = [[chip * CO + core for chip in range(XL * NZ)] for core in range(CO)]
    column = lax.all_to_all(chosen, "arc", 0, 0, axis_index_groups=same_core, tiled=True)
    column, own, far = tie((column, own, far))
    (own[-3], own[3]), far[1] = third, second
    near, across = {0: turn(column)}, {}
    near[-1], near[1], across[0] = send(near[0], dy=1), send(near[0], dy=-1), send(near[0], dxh=1)
    own[-3], own[3], far[0], far[1] = tie((own[-3], own[3], far[0], far[1]))
    far[-1], own[4] = send(far[0], dz=1), send(own[3], dz=-1)
    far[-1], near[-1], near[1], own[4] = tie((far[-1], near[-1], near[1], own[4]))
    across[0], beside = tie((across[0], own[3]))
    far[3] = send(beside, dxl=1)
    across[-1], across[1] = send(across[0], dy=1), send(across[0], dy=-1)
    across[-1], beside = tie((across[-1], near[-1]))
    near[2] = send(beside, dy=1)
    far[-2], far[2] = send(far[-1], dz=1), send(far[1], dz=-1)
    across[1], far[3] = tie((across[1], far[3]))
    across[2] = send(across[1], dy=-1)
    left = [(near, across)[dxh][dy if dy <= 2 else dy - 4] for dy, dxh in EARLY]
    stacked, picked, far[-2] = tie((stack_early(left), pick_late(left), far[-2]))
    far[-3], far[4] = send(far[-2], dz=1), send(own[4], dxl=1)
    own[3], own[-3], far[1] = bring((own[3], own[-3], far[1]))
    right = [group[d if d <= 4 else d - 8] for group in (own, far) for d in range(NZ)]
    cuts = ((0, 1280), (1280, WIDE))
    ready = right[: LATE[0]] + right[LATE[-1] + 1 :]
    sums = [early_product(stacked, ready, *cut) for cut in cuts]
    late = [right[i] for i in LATE]
    last, late, sums = tie(([near[2], across[2]], late, sums))
    right[LATE[0] : LATE[-1] + 1] = late
    mine_a, other_a = late_product(last, picked, right, *cuts[0], sums[0])
    passed_a = send(other_a, dcore=1)
    mine_b, other_b = late_product(last, picked, right, *cuts[1], sums[1])
    passed_b = send(other_b, dcore=1)
    whole = finish(mine_a, passed_a, *cuts[0])
    return finish(mine_b, passed_b, *cuts[1], whole)


def solution(mesh):
    in_specs = (P(None, "arc", "col"), P(None, None, "arc"), P(None, "arc"), P("arc"), P(), P())
    out_specs = P("arc", "col")
    return jax.shard_map(body, mesh=mesh, in_specs=in_specs, out_specs=out_specs, check_vma=False)
```

```python
import functools

import jax
import jax.numpy as jnp
from jax import lax
from jax.experimental import pallas as pl
from jax.experimental.pallas import tpu as pltpu
from jax.sharding import PartitionSpec as P

HIGH = lax.Precision.HIGHEST
AXES = ("arc", "col")
XL, NZ, CO, NY, XH = 2, 8, 2, 4, 2
EPOCHS = 64
SLOTS = 8
WIDE = 1920
BLOCK = 480
EVERY = 2048
LAST = [(2, 0), (2, 1)]
EARLY = [(dy, dxh) for dy in (0, 1, 3) for dxh in range(XH)]
LATE = (NZ + 4, NZ + 5)
DEEP = 128 * len(LAST)
PICK = SLOTS * len(LATE) * len(EARLY)
MIB = 1 << 20
WHOLE = 60 * MIB
VMEM = pl.BlockSpec(memory_space=pltpu.VMEM)
SMEM = pl.BlockSpec(memory_space=pltpu.SMEM)
HBM = pl.BlockSpec(memory_space=pltpu.HBM)


def place(device):
    arc, col = divmod(device, NY * XH)
    xl, rest = divmod(arc, NZ * CO)
    z, core = divmod(rest, CO)
    y, xh = divmod(col, XH)
    return xl, z, core, y, xh


def number(xl, z, core, y, xh):
    return (((xl * NZ + z) * CO + core) * NY + y) * XH + xh


def send(value, dxl=0, dz=0, dcore=0, dy=0, dxh=0):
    pairs = []
    for device in range(XL * NZ * CO * NY * XH):
        xl, z, core, y, xh = place(device)
        there = number(xl ^ dxl, (z + dz) % NZ, core ^ dcore, (y + dy) % NY, xh ^ dxh)
        pairs.append((device, there))
    return lax.ppermute(value, AXES, pairs)


def coordinates():
    arc, col = lax.axis_index("arc"), lax.axis_index("col")
    xl, z, core = arc // (NZ * CO), (arc // CO) % NZ, arc % CO
    return xl, z, core, col // XH, col % XH


def scan_kernel(
    lengths_hbm, propagate_hbm, sight_hbm, weights_hbm, force_hbm,
    pack, coef, flat,
    lengths, propagate, sight, weights, keep, last, sems,
):
    loads = [
        pltpu.make_async_copy(force_hbm, flat, sems.at[0]),
        pltpu.make_async_copy(lengths_hbm, lengths, sems.at[1]),
        pltpu.make_async_copy(propagate_hbm, propagate, sems.at[2]),
        pltpu.make_async_copy(sight_hbm, sight, sems.at[3]),
        pltpu.make_async_copy(weights_hbm, weights, sems.at[4]),
    ]
    for load in loads:
        load.start()
    rank = lax.axis_index("arc")

    def clear(t, _):
        keep[t] = 1.0
        return 0

    lax.fori_loop(0, EPOCHS, clear, 0)
    loads[1].wait()

    def mark(arc, start):
        local = start - rank * EPOCHS

        @pl.when((local >= 0) & (local < EPOCHS))
        def _():
            keep[local] = 0.0

        return start + lengths[arc]

    lax.fori_loop(0, lengths.shape[0], mark, jnp.int32(0))
    lane = lax.broadcasted_iota(jnp.int32, (1, 256), 1)
    rows = tuple((lane == 192 + i).astype(jnp.float32) for i in range(6))
    loads[2].wait()
    loads[3].wait()
    loads[4].wait()

    def step(t, rows):
        live = keep[t]
        kicked = []
        for i in range(6):
            total = propagate[i, 0, t] * rows[0]
            for j in range(1, 6):
                total = total + propagate[i, j, t] * rows[j]
            kick = jnp.where(lane == (i % 3) * EPOCHS + t, 0.5 if i < 3 else 1.0, 0.0)
            kicked.append(live * total + kick)
        seen = sight[0, t] * kicked[0]
        for i in range(1, 6):
            seen = seen + sight[i, t] * kicked[i]
        coef[pl.ds(t, 1), :] = jnp.where(lane == 200, weights[t] / EVERY, seen)
        return tuple(kicked)

    rows = lax.fori_loop(0, EPOCHS, step, rows, unroll=4)
    last[...] = jnp.zeros_like(last)
    for i in range(6):
        last[i : i + 1, :] = rows[i]
    loads[0].wait()
    pack[:, :WIDE] = jnp.dot(
        last[:, : 3 * EPOCHS],
        flat[...].reshape(3 * EPOCHS, WIDE),
        precision=HIGH,
        preferred_element_type=jnp.float32,
    )
    pack[:, WIDE:] = last[:, 128:]


def scan(lengths, propagate, sight, weights, force):
    return pl.pallas_call(
        scan_kernel,
        out_shape=(
            jax.ShapeDtypeStruct((8, WIDE + 128), jnp.float32),
            jax.ShapeDtypeStruct((EPOCHS, 256), jnp.float32),
            jax.ShapeDtypeStruct(force.shape, jnp.float32),
        ),
        in_specs=[HBM] * 5,
        out_specs=(VMEM, VMEM, VMEM),
        scratch_shapes=[
            pltpu.SMEM(lengths.shape, jnp.int32),
            pltpu.SMEM(propagate.shape, jnp.float32),
            pltpu.SMEM(sight.shape, jnp.float32),
            pltpu.SMEM(weights.shape, jnp.float32),
            pltpu.SMEM((EPOCHS,), jnp.float32),
            pltpu.VMEM((8, 256), jnp.float32),
            pltpu.SemaphoreType.DMA((5,)),
        ],
        compiler_params=pltpu.CompilerParams(vmem_limit_bytes=WHOLE),
        name="scan",
    )(lengths, propagate, sight, weights, force)


def local_kernel(coef, flat, design):
    design[...] = jnp.dot(
        coef[:, : 3 * EPOCHS],
        flat[...].reshape(3 * EPOCHS, WIDE),
        precision=HIGH,
        preferred_element_type=jnp.float32,
    )


def local_design(coef, flat):
    return pl.pallas_call(
        local_kernel,
        out_shape=jax.ShapeDtypeStruct((EPOCHS, WIDE), jnp.float32),
        in_specs=[VMEM, VMEM],
        out_specs=VMEM,
        compiler_params=pltpu.CompilerParams(vmem_limit_bytes=16 * MIB),
        cost_estimate=pl.CostEstimate(flops=300_000_000, bytes_accessed=2_000_000, transcendentals=0),
        name="local",
    )(coef, flat)


def apply(matrix, state):
    total = matrix[:, 0:1] * state[0:1, :]
    for j in range(1, 6):
        total = total + matrix[:, j : j + 1] * state[j : j + 1, :]
    return total


def design_kernel(one, two, three, coef, local, design, keep, cross, weighted):
    state = three[:, :WIDE]
    for earlier in (two, one):
        state = apply(earlier[:, WIDE + 64 : WIDE + 70], state) + earlier[:, :WIDE]
    full = local[...] + apply(coef[:, 192:198], state)
    design[...] = full
    weighted[...] = full * coef[:, 200:201]
    _, _, _, y, xh = coordinates()
    for dy in range(NY):
        for dxh, out in enumerate((keep, cross)):
            slot = lax.rem(y + dy, NY) * XH + lax.rem(xh + dxh, XH)
            out[dy] = weighted[pl.ds(pl.multiple_of(slot * SLOTS, SLOTS), SLOTS), :]


def full_design(one, two, three, coef, local):
    pieces = jax.ShapeDtypeStruct((NY, SLOTS, WIDE), jnp.float32)
    return pl.pallas_call(
        design_kernel,
        out_shape=(jax.ShapeDtypeStruct((EPOCHS, WIDE), jnp.float32), pieces, pieces),
        in_specs=[VMEM] * 5,
        out_specs=(VMEM, VMEM, VMEM),
        scratch_shapes=[pltpu.VMEM((EPOCHS, WIDE), jnp.float32)],
        compiler_params=pltpu.CompilerParams(vmem_limit_bytes=16 * MIB),
        name="design",
    )(one, two, three, coef, local)


def pair_kernel(first, second, *outs):
    for i, out in enumerate(outs):
        out[0] = first[i]
        out[1] = second[i]


def pair(first, second):
    out = jax.ShapeDtypeStruct((2,) + first.shape[1:], jnp.float32)
    return pl.pallas_call(
        pair_kernel,
        out_shape=(out,) * first.shape[0],
        in_specs=[VMEM, VMEM],
        out_specs=(VMEM,) * first.shape[0],
        compiler_params=pltpu.CompilerParams(vmem_limit_bytes=16 * MIB),
        cost_estimate=pl.CostEstimate(flops=5_000_000_000, bytes_accessed=1_000_000, transcendentals=0),
        name="pair",
    )(first, second)


def choose_kernel(order, *refs):
    pieces, out, blocks = refs[:4], refs[4], refs[5]
    _, _, core, y, xh = coordinates()
    for dy in range(NY):
        for dxh in range(XH):
            col = lax.rem(y + dy, NY) * XH + lax.rem(xh + dxh, XH)
            for j in range(4):
                blocks[4 * col + j] = pieces[dy][dxh, :, BLOCK * j : BLOCK * (j + 1)]
    for chip in range(XL * NZ):
        for dcore in range(CO):
            out[chip, dcore] = blocks[order[chip * CO + lax.rem(core + dcore, CO)]]


def choose(order, pieces):
    return pl.pallas_call(
        choose_kernel,
        out_shape=jax.ShapeDtypeStruct((XL * NZ, CO, SLOTS, BLOCK), jnp.float32),
        in_specs=[SMEM] + [VMEM] * 4,
        out_specs=VMEM,
        scratch_shapes=[pltpu.VMEM((32, SLOTS, BLOCK), jnp.float32)],
        compiler_params=pltpu.CompilerParams(vmem_limit_bytes=16 * MIB),
        name="choose",
    )(order, *pieces)


def turn_kernel(pieces, out, gathered):
    xl, z, _, _, _ = coordinates()
    for dcore in range(CO):
        for dxl in range(XL):
            for dz in range(NZ):
                chip = lax.rem(xl + dxl, XL) * NZ + lax.rem(z + dz, NZ)
                start = SLOTS * (dxl * NZ + dz)
                gathered[start : start + SLOTS, :BLOCK] = pieces[chip, dcore]
        out[BLOCK * dcore : BLOCK * (dcore + 1), :] = jnp.transpose(gathered[...])[:BLOCK]


def turn(pieces):
    return pl.pallas_call(
        turn_kernel,
        out_shape=jax.ShapeDtypeStruct((CO * BLOCK, 128), jnp.float32),
        in_specs=[VMEM],
        out_specs=VMEM,
        scratch_shapes=[pltpu.VMEM((128, 512), jnp.float32)],
        compiler_params=pltpu.CompilerParams(vmem_limit_bytes=16 * MIB),
        name="turn",
    )(pieces)


def split(value):
    high = value.astype(jnp.bfloat16)
    return high, (value - high.astype(jnp.float32)).astype(jnp.bfloat16)


def stack_kernel(*refs):
    left, out = refs[:-1], refs[-1]
    depth = 128 * len(left)
    for j, shard in enumerate(left):
        high, low = split(shard[...])
        for part, value in enumerate((high, low, high)):
            out[:, depth * part + 128 * j : depth * part + 128 * (j + 1)] = value


def stack_early(left):
    return pl.pallas_call(
        stack_kernel,
        out_shape=jax.ShapeDtypeStruct((CO * BLOCK, 3 * 128 * len(left)), jnp.bfloat16),
        in_specs=[VMEM] * len(left),
        out_specs=VMEM,
        compiler_params=pltpu.CompilerParams(vmem_limit_bytes=12 * MIB),
        name="stack",
    )(*left)


def pick_kernel(*refs):
    left, out = refs[:-1], refs[-1]
    lanes = slice(SLOTS * LATE[0], SLOTS * (LATE[-1] + 1))
    value = jnp.concatenate([shard[:, lanes] for shard in left], axis=1)
    high = value.astype(jnp.bfloat16).astype(jnp.float32)
    parts = [high, value - high, high, jnp.zeros_like(high)]
    out[...] = jnp.concatenate(parts, axis=1).astype(jnp.bfloat16)


def pick_late(left):
    return pl.pallas_call(
        pick_kernel,
        out_shape=jax.ShapeDtypeStruct((CO * BLOCK, 4 * PICK), jnp.bfloat16),
        in_specs=[VMEM] * len(left),
        out_specs=VMEM,
        compiler_params=pltpu.CompilerParams(vmem_limit_bytes=12 * MIB),
        name="pick",
    )(*left)


def bring_kernel(*refs):
    half = len(refs) // 2
    for source, target in zip(refs[:half], refs[half:]):
        target[...] = source[...]


def bring(values):
    return pl.pallas_call(
        bring_kernel,
        out_shape=tuple(jax.ShapeDtypeStruct(value.shape, value.dtype) for value in values),
        in_specs=[VMEM] * len(values),
        out_specs=(VMEM,) * len(values),
        compiler_params=pltpu.CompilerParams(vmem_limit_bytes=12 * MIB),
        name="bring",
    )(*values)


def slot_rows(dy, dxh):
    _, _, _, y, xh = coordinates()
    slot = lax.rem(y + dy, NY) * XH + lax.rem(xh + dxh, XH)
    return pl.ds(pl.multiple_of(slot * SLOTS, SLOTS), SLOTS)


def early_kernel(lo, hi, left, *refs):
    right, outs, stacked = refs[:14], refs[14:16], refs[16]
    depth = 128 * len(EARLY)
    none = jnp.zeros((SLOTS * len(LATE), hi - lo), jnp.float32)
    for j, place in enumerate(EARLY):
        rows = slot_rows(*place)
        chunk = [block[rows, lo:hi] for block in right]
        high, low = split(jnp.concatenate(chunk[: LATE[0]] + [none] + chunk[LATE[0] :], axis=0))
        for part, value in enumerate((high, high, low)):
            stacked[depth * part + 128 * j : depth * part + 128 * (j + 1), :] = value
    for i, out in enumerate(outs):
        out[...] = jnp.dot(
            left[BLOCK * i : BLOCK * (i + 1), :], stacked[...], preferred_element_type=jnp.float32
        )


def early_product(left, right, lo, hi):
    out = jax.ShapeDtypeStruct((BLOCK, hi - lo), jnp.float32)
    depth = 128 * len(EARLY)
    return pl.pallas_call(
        functools.partial(early_kernel, lo, hi),
        out_shape=(out, out),
        in_specs=[VMEM] * 15,
        out_specs=(VMEM, VMEM),
        scratch_shapes=[pltpu.VMEM((3 * depth, hi - lo), jnp.bfloat16)],
        compiler_params=pltpu.CompilerParams(vmem_limit_bytes=14 * MIB),
        cost_estimate=pl.CostEstimate(
            flops=12 * BLOCK * depth * (hi - lo), bytes_accessed=14_000_000, transcendentals=0
        ),
        name="early",
    )(left, *right)


def late_kernel(lo, hi, first, second, picked, *refs):
    right, sums, outs, across, stacked = refs[:16], refs[16:18], refs[18:20], refs[20], refs[21]
    for j, (place, shard) in enumerate(zip(LAST, (first, second))):
        high, low = split(shard[...])
        for part, value in enumerate((high, low, high)):
            across[:, DEEP * part + 128 * j : DEEP * part + 128 * (j + 1)] = value
        rows = slot_rows(*place)
        high, low = split(jnp.concatenate([block[rows, lo:hi] for block in right], axis=0))
        for part, value in enumerate((high, high, low)):
            stacked[DEEP * part + 128 * j : DEEP * part + 128 * (j + 1), :] = value
    across[:, 3 * DEEP :] = picked[...]
    pieces = [right[i][slot_rows(*place), lo:hi] for place in EARLY for i in LATE]
    high, low = split(jnp.concatenate(pieces, axis=0))
    for part, value in enumerate((high, high, low, jnp.zeros_like(low))):
        stacked[3 * DEEP + PICK * part : 3 * DEEP + PICK * (part + 1), :] = value
    for i, out in enumerate(outs):
        out[...] = sums[i][...] + jnp.dot(
            across[BLOCK * i : BLOCK * (i + 1), :], stacked[...], preferred_element_type=jnp.float32
        )


def late_product(left, picked, right, lo, hi, sums):
    out = jax.ShapeDtypeStruct((BLOCK, hi - lo), jnp.float32)
    depth = 3 * DEEP + 4 * PICK
    return pl.pallas_call(
        functools.partial(late_kernel, lo, hi),
        out_shape=(out, out),
        in_specs=[VMEM] * 21,
        out_specs=(VMEM, VMEM),
        scratch_shapes=[
            pltpu.VMEM((CO * BLOCK, depth), jnp.bfloat16),
            pltpu.VMEM((depth, hi - lo), jnp.bfloat16),
        ],
        compiler_params=pltpu.CompilerParams(vmem_limit_bytes=14 * MIB),
        cost_estimate=pl.CostEstimate(
            flops=4 * BLOCK * depth * (hi - lo), bytes_accessed=14_000_000, transcendentals=0
        ),
        name="late",
    )(*left, picked, *right, *sums)


def finish_kernel(lo, hi, mine, passed, *refs):
    out, total, sem = refs[-3:]
    total[...] = mine[...] + passed[...]
    copy = pltpu.make_async_copy(total, out.at[:, lo:hi], sem)
    copy.start()
    copy.wait()


def finish(mine, passed, lo, hi, whole=None):
    given = () if whole is None else (whole,)
    return pl.pallas_call(
        functools.partial(finish_kernel, lo, hi),
        out_shape=jax.ShapeDtypeStruct((BLOCK, WIDE), jnp.float32),
        in_specs=[VMEM, VMEM] + [HBM] * len(given),
        out_specs=HBM,
        scratch_shapes=[pltpu.VMEM((BLOCK, hi - lo), jnp.float32), pltpu.SemaphoreType.DMA],
        input_output_aliases={2: 0} if given else {},
        compiler_params=pltpu.CompilerParams(vmem_limit_bytes=16 * MIB),
        name="finish",
    )(mine, passed, *given)


def shift_arc(value, step):
    arcs, cols = XL * NZ * CO, NY * XH
    pairs = [
        (arc * cols + col, (arc + step) * cols + col)
        for arc in range(arcs - step)
        for col in range(cols)
    ]
    return lax.ppermute(value, AXES, pairs)


def body(force, propagate, sight, weights, lengths, order):
    tie = lax.optimization_barrier
    pack, coef, flat = scan(lengths, propagate, sight, weights, force)
    before = [shift_arc(pack, step) for step in (1, 2, 3)]
    design, keep, cross = full_design(*before, coef, local_design(coef, flat))
    own, far = {0: design}, {}
    got, beside = tie((send(cross, dxh=1), own[0]))
    own[-1], own[1] = send(own[0], dz=1), send(own[0], dz=-1)
    to = pair(keep, got)
    rows = [to[0], send(to[3], dy=-1), send(to[2], dy=2), send(to[1], dy=1)]
    rows, own = tie((rows, own))
    own[-2], own[2] = send(own[-1], dz=1), send(own[1], dz=-1)
    third = send(own[-2], dz=1), send(own[2], dz=-1)
    far[0], beside = tie((send(beside, dxl=1), own[1]))
    second = send(beside, dxl=1)
    chosen = choose(order, rows)
    same_core = [[chip * CO + core for chip in range(XL * NZ)] for core in range(CO)]
    column = lax.all_to_all(chosen, "arc", 0, 0, axis_index_groups=same_core, tiled=True)
    column, own, far = tie((column, own, far))
    (own[-3], own[3]), far[1] = third, second
    near, across = {0: turn(column)}, {}
    near[-1], near[1], across[0] = send(near[0], dy=1), send(near[0], dy=-1), send(near[0], dxh=1)
    own[-3], own[3], far[0], far[1] = tie((own[-3], own[3], far[0], far[1]))
    far[-1], own[4] = send(far[0], dz=1), send(own[3], dz=-1)
    far[-1], near[-1], near[1], own[4] = tie((far[-1], near[-1], near[1], own[4]))
    across[0], beside = tie((across[0], own[3]))
    far[3] = send(beside, dxl=1)
    across[-1], across[1] = send(across[0], dy=1), send(across[0], dy=-1)
    across[-1], beside = tie((across[-1], near[-1]))
    near[2] = send(beside, dy=1)
    far[-2], far[2] = send(far[-1], dz=1), send(far[1], dz=-1)
    across[1], far[3] = tie((across[1], far[3]))
    across[2] = send(across[1], dy=-1)
    left = [(near, across)[dxh][dy if dy <= 2 else dy - 4] for dy, dxh in EARLY]
    stacked, picked, far[-2] = tie((stack_early(left), pick_late(left), far[-2]))
    far[-3], far[4] = send(far[-2], dz=1), send(own[4], dxl=1)
    own[3], own[-3], far[1] = bring((own[3], own[-3], far[1]))
    right = [group[d if d <= 4 else d - 8] for group in (own, far) for d in range(NZ)]
    cuts = ((0, 1280), (1280, WIDE))
    ready = right[: LATE[0]] + right[LATE[-1] + 1 :]
    sums = [early_product(stacked, ready, *cut) for cut in cuts]
    late = [right[i] for i in LATE]
    last, late, sums = tie(([near[2], across[2]], late, sums))
    right[LATE[0] : LATE[-1] + 1] = late
    mine_a, other_a = late_product(last, picked, right, *cuts[0], sums[0])
    passed_a = send(other_a, dcore=1)
    mine_b, other_b = late_product(last, picked, right, *cuts[1], sums[1])
    passed_b = send(other_b, dcore=1)
    whole = finish(mine_a, passed_a, *cuts[0])
    return finish(mine_b, passed_b, *cuts[1], whole)


def solution(mesh):
    in_specs = (P(None, "arc", "col"), P(None, None, "arc"), P(None, "arc"), P("arc"), P(), P())
    out_specs = P("arc", "col")
    return jax.shard_map(body, mesh=mesh, in_specs=in_specs, out_specs=out_specs, check_vma=False)
```
